32 devices in a mesh: dp: 8 (over z, x), block: 4 (over y, core).
Axes of the slice: x: 2, y: 2, z: 4, core: 2. Of those that a mesh axis runs over, the one named last changes fastest.
Arguments:
- inputs: bfloat16 [3072, 2048], P('dp', 'block'), may hold values from -6 to 6
- weight_in: bfloat16 [512, 3, 4096], P('dp', None, 'block'), may hold values from -0.15625 to 0.15625
- weight_out: bfloat16 [1024, 3, 2048], P('dp', None, 'block'), may hold values from -0.109375 to 0.109375
- cotangent: bfloat16 [3072, 2048], P('dp', 'block'), may hold values from -6 to 6
Outputs:
- outputs: bfloat16 [3072, 2048], P('dp', 'block')
- input_grad: bfloat16 [3072, 2048], P('dp', 'block')
- grad_in: float32 [512, 3, 4096], P('dp', None, 'block')
- grad_out: float32 [1024, 3, 2048], P('dp', None, 'block')
The draws below stay inside these ranges and needn't reach their ends.
All inputs are finite; a program needn't handle non-finite values.
Results may differ from the reference program's by a relative error of at most 0.017.
Values may be sent and summed in bfloat16 or wider, within the bound.
A program may use at most 128 MiB of HBM per device.

```python
import jax
import jax.numpy as jnp
from jax import lax

BW = 512
HP = 1024
TOK_DEV = 384
LEVELS = 2
D = 2048
H = 4096
TOKENS = 3072
N_DP = 8
N_BLOCK = 4


def shard_levels(stream_key, shape, cuts, least, high):
    def one(position, parts):
        heights = jax.random.uniform(jax.random.fold_in(jax.random.fold_in(stream_key, 6), position), (parts,), jnp.float32, least / len(cuts), high / len(cuts))
        return jnp.repeat(jnp.exp(heights), shape[position] // parts).reshape((-1,) + (1,) * (len(shape) - position - 1))

    loudness = one(*cuts[0])
    for cut in cuts[1:]:
        loudness = loudness * one(*cut)
    return loudness


def noise(key, dims, deviation, bound, pieces=(), dtype=jnp.bfloat16):
    entries = deviation * jax.random.normal(key, dims, jnp.float32)
    if pieces:
        entries = entries * shard_levels(key, dims, pieces, -0.22, 0.18)
    return jnp.clip(entries, -bound, bound).astype(dtype)


def setup_inputs(seed: int = 0) -> dict:
    arg_keys = jax.random.split(jax.random.key(seed), 5)
    return {
        "inputs": noise(arg_keys[0], (TOKENS, D), 1.0, 6.0, ((0, 8), (1, 4))),
        "weight_in": noise(arg_keys[1], (BW, LEVELS + 1, H), (BW * (LEVELS + 1)) ** -0.5, 0.15625, ((0, 8), (2, 4))),
        "weight_out": noise(arg_keys[2], (HP, LEVELS + 1, D), (HP * (LEVELS + 1)) ** -0.5, 0.109375, ((0, 8), (2, 4))),
        "cotangent": noise(arg_keys[3], (TOKENS, D), 1.0, 6.0, ((0, 8), (1, 4))),
    }


def distance(level):
    return 0 if level == 0 else 1 << level - 1

def cut(array, index, width):
    return array[:, index * width:(index + 1) * width]

def rounded(value):
    return lax.optimization_barrier(value.astype(jnp.bfloat16)).astype(jnp.float32)

def gelu_tanh(value):
    return jax.nn.gelu(value, approximate=True)

def token_sum(left, right):
    left_rows = left.reshape(N_DP, TOK_DEV, left.shape[1]).astype(jnp.float32)
    right_rows = right.reshape(N_DP, TOK_DEV, right.shape[1]).astype(jnp.float32)
    partial_sums = jnp.einsum('rta,rtb->rab', left_rows, right_rows, precision=lax.Precision.HIGHEST)
    return lax.optimization_barrier(jnp.sum(rounded(partial_sums), axis=0))

def reference(inputs, weight_in, weight_out, cotangent):
    hid_grads = []
    for panel in range(N_BLOCK):
        total = jnp.zeros((TOKENS, HP), jnp.float32)
        for level in range(LEVELS + 1):
            source = panel ^ distance(level)
            term = jnp.dot(cut(cotangent, source, BW), cut(weight_out[:, level, :], source, BW).T, preferred_element_type=jnp.float32)
            total = total + rounded(term)
        hid_grads.append(total)
    hiddens = []
    pre_grads = []
    for panel in range(N_BLOCK):
        pre_act = jnp.zeros((TOKENS, HP), jnp.float32)
        for level in range(LEVELS + 1):
            source = panel ^ distance(level)
            pre_act = pre_act + jnp.dot(cut(inputs, source, BW), cut(weight_in[:, level, :], panel, HP), preferred_element_type=jnp.float32)
        hiddens.append(gelu_tanh(pre_act).astype(jnp.bfloat16))
        slope = jax.vjp(gelu_tanh, pre_act)[1](hid_grads[panel])[0]
        pre_grads.append(slope.astype(jnp.bfloat16))
    out_blocks = []
    grad_blocks = []
    for block in range(N_BLOCK):
        total = jnp.zeros((TOKENS, BW), jnp.float32)
        back = jnp.zeros((TOKENS, BW), jnp.float32)
        for level in range(LEVELS + 1):
            source = block ^ distance(level)
            total = total + jnp.dot(hiddens[source], cut(weight_out[:, level, :], block, BW), preferred_element_type=jnp.float32)
            term = jnp.dot(pre_grads[source], cut(weight_in[:, level, :], source, HP).T, preferred_element_type=jnp.float32)
            back = back + rounded(term)
        out_blocks.append(total.astype(jnp.bfloat16))
        grad_blocks.append(back.astype(jnp.bfloat16))
    outputs = jnp.concatenate(out_blocks, axis=1)
    input_grad = jnp.concatenate(grad_blocks, axis=1)
    in_levels = []
    out_levels = []
    for level in range(LEVELS + 1):
        in_levels.append(jnp.concatenate([token_sum(cut(inputs, panel ^ distance(level), BW), pre_grads[panel]) for panel in range(N_BLOCK)], axis=1))
        out_levels.append(jnp.concatenate([token_sum(hiddens[block ^ distance(level)], cut(cotangent, block, BW)) for block in range(N_BLOCK)], axis=1))
    grad_in = jnp.stack(in_levels, axis=1)
    grad_out = jnp.stack(out_levels, axis=1)
    return (outputs, input_grad, grad_in, grad_out)
```

```python
import functools

import jax
import jax.numpy as jnp
from jax import lax
from jax.experimental import pallas as pl
from jax.experimental.pallas import tpu as pltpu
from jax.sharding import PartitionSpec as P

MESH = pl.DeviceIdType.MESH
F32, BF16 = jnp.float32, jnp.bfloat16
GELU_C, GELU_A = 0.7978845608028654, 0.044715


def dot(a, b, ca, cb):
    return lax.dot_general(a, b, (((ca,), (cb,)), ((), ())), preferred_element_type=F32)


def tiles(total, size, step):
    size = min(size, total)

    def one(i, carry):
        step(pl.ds(pl.multiple_of(i * size, size), size))
        return carry

    lax.fori_loop(0, total // size, one, 0)


def kernel(
    Z, X, L, x_ref, ct_ref, wi_ref, wo_ref, out_ref, ig_ref, gi_ref, go_ref,
    wo, wi, xg, cg, ht_own, ht_send, ht_recv, hg, pg, gi_send, gi_recv, go_send, go_recv,
    ig_send, ig_recv, o_send, o_recv,
    wo_s, wo_r, wi_s, wi_r, x_s, x_r, ct_s, ct_r, ht_s, ht_r, hg_s, hg_r, gi_s, gi_r, go_s, go_r,
    ig_s, ig_r, o_s, o_r,
):
    dp, b = lax.axis_index("dp"), lax.axis_index("block")
    z, x = dp // X, dp % X
    T, C = x_ref.shape
    R1, R2 = wi_ref.shape[2], wo_ref.shape[1]
    TX, HX = X * T, Z * R2

    def flip(k):
        if k == 0:
            return b
        d = 2 ** (k - 1)
        return b + d - 2 * d * ((b // d) % 2)

    def zat(o):
        return (z + o) % Z

    def xat(o):
        return (x + o) % X

    grid = [(oz, ox) for oz in range(Z) for ox in range(X) if oz or ox]
    near = [(ox, k) for k in reversed(range(L)) for ox in range(X) if ox or k]
    rows_t = pl.ds(pl.multiple_of(x * T, T), T)
    rows_1 = pl.ds(pl.multiple_of(dp * R1, R1), R1)
    rows_2 = pl.ds(pl.multiple_of(z * R2, R2), R2)

    sent = []

    def send(src, dst, ssem, rsem, zd, xd, bd):
        c = pltpu.make_async_remote_copy(
            src_ref=src, dst_ref=dst, send_sem=ssem, recv_sem=rsem,
            device_id=(zd * X + xd, bd), device_id_type=MESH,
        )
        c.start()
        sent.append(c)
        return c

    barrier = pltpu.get_barrier_semaphore()
    for oz, ox in grid:
        pl.semaphore_signal(barrier, inc=1, device_id=(zat(oz) * X + xat(ox), b), device_id_type=MESH)
    for ox, k in near:
        if k:
            pl.semaphore_signal(barrier, inc=1, device_id=(z * X + xat(ox), flip(k)), device_id_type=MESH)
    wo[:, rows_2, :] = wo_ref[...]
    wi[:, rows_1, :] = wi_ref[x]
    xg[0, rows_t, :] = x_ref[...]
    cg[rows_t, :] = ct_ref[...]
    pl.semaphore_wait(barrier, len(grid) + X * (L - 1))

    wo_c = [
        send(wo_ref, wo.at[:, rows_2, :], wo_s.at[o], wo_r.at[o], zat(o), x, b)
        for o in range(1, Z)
    ]
    ct_c = [
        send(ct_ref, cg.at[rows_t, :], ct_s.at[o], ct_r.at[o], z, xat(o), b) for o in range(1, X)
    ]
    x_c = [
        send(x_ref, xg.at[k, rows_t, :], x_s.at[ox, k], x_r.at[ox, k], z, xat(ox), flip(k))
        for ox, k in near
    ]
    wi_c = [
        send(wi_ref.at[xat(ox)], wi.at[:, rows_1, :], wi_s.at[oz, ox], wi_r.at[oz, ox], zat(oz), xat(ox), b)
        for oz, ox in grid
    ]

    for c in ct_c + wo_c:
        c.wait_recv()
    ht_c = []
    for k in reversed(range(L)):

        def back(rows, k=k):
            term = dot(cg[rows, :], wo[k], 1, 1).astype(BF16)
            if k:
                ht_send[k - 1, rows, :] = term
            else:
                ht_own[rows, :] = term

        tiles(TX, 256, back)
        if k:
            ht_c.append(
                send(ht_send.at[k - 1], ht_recv.at[k - 1], ht_s.at[k], ht_r.at[k], z, x, flip(k))
            )

    for c in x_c + wi_c + ht_c:
        c.wait_recv()

    def middle(rows):
        v = dot(xg[0, rows, :], wi[0], 1, 0)
        for k in range(1, L):
            v = v + dot(xg[k, rows, :], wi[k], 1, 0)
        g = ht_own[rows, :].astype(F32)
        for k in range(1, L):
            g = g + ht_recv[k - 1, rows, :].astype(F32)
        v2 = v * v
        t = jnp.tanh(GELU_C * v * (1.0 + GELU_A * v2))
        half = 0.5 + 0.5 * t
        hg[0, rows, :] = (v * half).astype(BF16)
        slope = half + 0.5 * v * (1.0 - t * t) * (GELU_C * (1.0 + 3.0 * GELU_A * v2))
        pg[rows, :] = (g * slope).astype(BF16)

    tiles(TX, 128, middle)
    hg_c = [
        send(hg.at[0], hg.at[k], hg_s.at[k], hg_r.at[k], z, x, flip(k))
        for k in reversed(range(1, L))
    ]

    for k in range(L):

        def grad_in(rows, k=k):
            gi_send[k, rows, :] = dot(xg[k, :, rows], pg[...], 0, 0).astype(BF16)

        tiles(C, 256, grad_in)
    gi_c = [
        send(
            gi_send.at[:, pl.ds(pl.multiple_of((zat(oz) * X + xat(ox)) * R1, R1), R1), :],
            gi_recv.at[oz, ox], gi_s.at[oz, ox], gi_r.at[oz, ox], zat(oz), xat(ox), b,
        )
        for oz, ox in grid
    ]

    ig_c = []
    for k in reversed(range(L)):

        def grad_x(rows, k=k):
            ig_send[k, rows, :] = dot(pg[rows, :], wi[k], 1, 1).astype(BF16)

        tiles(TX, 256, grad_x)
        for ox in range(X):
            if ox or k:
                ig_c.append(
                    send(
                        ig_send.at[k, pl.ds(pl.multiple_of(xat(ox) * T, T), T), :],
                        ig_recv.at[k, ox], ig_s.at[ox, k], ig_r.at[ox, k], z, xat(ox), flip(k),
                    )
                )

    for k in range(L):
        if k:
            hg_c[L - 1 - k].wait_recv()

        def grad_out(rows, k=k):
            go_send[k, rows, :] = dot(hg[k, :, rows], cg[...], 0, 0).astype(BF16)

        tiles(HX, 256, grad_out)
    go_c = [
        send(
            go_send.at[:, pl.ds(pl.multiple_of(zat(o) * R2, R2), R2), :],
            go_recv.at[o], go_s.at[o], go_r.at[o], zat(o), x, b,
        )
        for o in range(1, Z)
    ]

    def forward(rows):
        total = dot(hg[0, rows, :], wo[0], 1, 0)
        for k in range(1, L):
            total = total + dot(hg[k, rows, :], wo[k], 1, 0)
        o_send[rows, :] = total.astype(BF16)

    tiles(TX, 256, forward)
    o_c = [
        send(
            o_send.at[pl.ds(pl.multiple_of(xat(o) * T, T), T), :],
            o_recv.at[o], o_s.at[o], o_r.at[o], z, xat(o), b,
        )
        for o in range(1, X)
    ]

    for c in ig_c:
        c.wait_recv()
    total = ig_send[0, rows_t, :].astype(F32)
    for ox, k in near:
        total = total + ig_recv[k, ox].astype(F32)
    ig_ref[...] = total.astype(BF16)
    for c in o_c:
        c.wait_recv()
    total = o_send[rows_t, :].astype(F32)
    for o in range(1, X):
        total = total + o_recv[o].astype(F32)
    out_ref[...] = total.astype(BF16)
    for c in gi_c:
        c.wait_recv()
    for k in range(L):
        for ox in range(X):
            if ox:
                total = gi_recv[0, ox, k].astype(F32)
            else:
                total = gi_send[k, rows_1, :].astype(F32)
            for oz in range(1, Z):
                total = total + gi_recv[oz, ox, k].astype(F32)
            gi_ref[(x + X - ox) % X, k] = total
    for c in go_c:
        c.wait_recv()
    for k in range(L):
        total = go_send[k, rows_2, :].astype(F32)
        for o in range(1, Z):
            total = total + go_recv[o, k].astype(F32)
        go_ref[k] = total
    for c in sent:
        c.wait_send()


def body(Z, X, inputs, weight_in, weight_out, cotangent):
    T, C = inputs.shape
    R1, L, panel = weight_in.shape
    R2 = weight_out.shape[0]
    TX, HX = X * T, Z * R2
    wi = weight_in.reshape(R1, L, Z, X, R2).transpose(3, 1, 0, 2, 4).reshape(X, L, R1, HX)
    wo = weight_out.transpose(1, 0, 2)
    vmem = pl.BlockSpec(memory_space=pltpu.VMEM)

    def buf(*shape):
        return pltpu.VMEM(shape, BF16)

    def sems(*shape):
        return [pltpu.SemaphoreType.DMA(shape)] * 2

    flops = 12 * TX * HX * C * L
    out, ig, gi, go = pl.pallas_call(
        functools.partial(kernel, Z, X, L),
        out_shape=(
            jax.ShapeDtypeStruct((T, C), BF16),
            jax.ShapeDtypeStruct((T, C), BF16),
            jax.ShapeDtypeStruct((X, L, R1, HX), F32),
            jax.ShapeDtypeStruct((L, R2, C), F32),
        ),
        in_specs=[vmem] * 4,
        out_specs=(vmem,) * 4,
        scratch_shapes=[
            buf(L, HX, C), buf(L, C, HX), buf(L, TX, C), buf(TX, C),
            buf(TX, HX), buf(L - 1, TX, HX), buf(L - 1, TX, HX),
            buf(L, TX, HX), buf(TX, HX),
            buf(L, C, HX), buf(Z, X, L, R1, HX), buf(L, HX, C), buf(Z, L, R2, C),
            buf(L, TX, C), buf(L, X, T, C), buf(TX, C), buf(X, T, C),
            *sems(Z), *sems(Z, X), *sems(X, L), *sems(X), *sems(L), *sems(L),
            *sems(Z, X), *sems(Z), *sems(X, L), *sems(X),
        ],
        compiler_params=pltpu.CompilerParams(
            collective_id=0, has_side_effects=True, vmem_limit_bytes=56 * 2**20
        ),
        cost_estimate=pl.CostEstimate(flops=flops, bytes_accessed=8 * 2**20, transcendentals=TX * HX),
    )(inputs, cotangent, wi, wo)
    grad_in = gi.reshape(X, L, R1, Z, R2).transpose(2, 1, 3, 0, 4).reshape(R1, L, panel)
    return out, ig, grad_in, go.transpose(1, 0, 2)


def solution(mesh):
    n = mesh.shape["dp"]
    Z = 4 if n % 4 == 0 else n
    placed = (P("dp", "block"), P("dp", None, "block"), P("dp", None, "block"), P("dp", "block"))
    return jax.shard_map(
        functools.partial(body, Z, n // Z),
        mesh=mesh,
        in_specs=placed,
        out_specs=(
            P("dp", "block"),
            P("dp", "block"),
            P("dp", None, "block"),
            P("dp", None, "block"),
        ),
        check_vma=False,
    )
```

```python
import functools

import jax
import jax.numpy as jnp
from jax import lax
from jax.experimental import pallas as pl
from jax.experimental.pallas import tpu as pltpu
from jax.sharding import PartitionSpec as P

MESH = pl.DeviceIdType.MESH
F32, BF16 = jnp.float32, jnp.bfloat16
GELU_C, GELU_A = 0.7978845608028654, 0.044715


def dot(a, b, ca, cb):
    return lax.dot_general(a, b, (((ca,), (cb,)), ((), ())), preferred_element_type=F32)


def tiles(total, size, step):
    size = min(size, total)

    def one(i, carry):
        step(pl.ds(pl.multiple_of(i * size, size), size))
        return carry

    lax.fori_loop(0, total // size, one, 0)


def kernel(
    Z, X, L, x_ref, ct_ref, wi_ref, wo_ref, out_ref, ig_ref, gi_ref, go_ref,
    wo, wi, xg, cg, pa, ht_own, ht_send, ht_recv, hg, pg, gi_part, gi_up, gi_dn, gx_send, gx_recv, acc,
    go_part, go_up, go_dn, ig_send, ig_recv, ig_sum, ig_x, o_send, o_recv,
    wo_us, wo_ur, wo_ds, wo_dr, wi_us, wi_ur, wi_ds, wi_dr, gi_us, gi_ur, gi_ds, gi_dr, go_us, go_ur, go_ds, go_dr,
    wx_s, wx_r, gx_s, gx_r, xx_s, xx_r, x_s, x_r, ct_s, ct_r, ht_s, ht_r, hg_s, hg_r, ig_s, ig_r, igx_s, igx_r, o_s, o_r,
):
    dp, b = lax.axis_index("dp"), lax.axis_index("block")
    z, x = dp // X, dp % X
    T, C = x_ref.shape
    R1, R2 = wi_ref.shape[2], wo_ref.shape[1]
    TX, HX, RX = X * T, Z * R2, X * R1

    def flip(k):
        d = 2 ** (k - 1)
        return b + d - 2 * d * ((b // d) % 2)

    def xat(o):
        return (x + o) % X

    def rows(index, size):
        return pl.ds(pl.multiple_of(index * size, size), size)

    rows_t = rows(x, T)
    rows_1 = rows(dp, R1)

    def copy(src, dst, ssem, rsem, zd, xd, bd):
        return pltpu.make_async_remote_copy(
            src_ref=src, dst_ref=dst, send_sem=ssem, recv_sem=rsem,
            device_id=(zd * X + xd, bd), device_id_type=MESH,
        )

    sent = []

    def send(*args):
        c = copy(*args)
        c.start()
        sent.append(c.wait_send)
        return c

    def send_if(cond, make):
        @pl.when(cond)
        def _():
            make().start()

        def done():
            @pl.when(cond)
            def _():
                make().wait_send()

        sent.append(done)

    WI = (wi, RX, wi_us, wi_ur, wi_ds, wi_dr)
    WO = (wo, R2, wo_us, wo_ur, wo_ds, wo_dr)

    def block(array, k, zz):
        return array[0].at[k, rows(zz, array[1]), :]

    def up(array, k, s):
        _, _, us, ur, _, _ = array
        send_if(
            jnp.logical_and(z >= s, z < Z - 1),
            lambda: copy(block(array, k, z - s), block(array, k, z - s), us.at[s, k], ur.at[s, k], z + 1, x, b),
        )

    def down(array, k, s):
        _, _, _, _, ds, dr = array
        send_if(
            jnp.logical_and(z + s < Z, z > 0),
            lambda: copy(block(array, k, z + s), block(array, k, z + s), ds.at[s, k], dr.at[s, k], z - 1, x, b),
        )

    def from_below(array, k, s):
        _, _, us, ur, _, _ = array

        @pl.when(z >= s + 1)
        def _():
            here = block(array, k, z - 1 - s)
            copy(here, here, us.at[s, k], ur.at[s, k], z - 1, x, b).wait_recv()

    def from_above(array, k, s):
        _, _, _, _, ds, dr = array

        @pl.when(z + 1 + s < Z)
        def _():
            here = block(array, k, z + 1 + s)
            copy(here, here, ds.at[s, k], dr.at[s, k], z + 1, x, b).wait_recv()

    def gather_start(array, k):
        up(array, k, 0)
        down(array, k, 0)

    def gather_pass(array, k):
        for s in range(Z - 2):
            from_below(array, k, s)
            up(array, k, s + 1)
            from_above(array, k, s)
            down(array, k, s + 1)

    def gather_end(array, k):
        from_below(array, k, Z - 2)
        from_above(array, k, Z - 2)

    GI = (gi_part, RX, gi_up, gi_dn, gi_us, gi_ur, gi_ds, gi_dr)
    GO = (go_part, R2, go_up, go_dn, go_us, go_ur, go_ds, go_dr)

    def add(array, k, d, here):
        part, size = array[0], array[1]
        r = pl.ds(d * size, size)
        part[k, r, :] = (part[k, r, :].astype(F32) + here[...].astype(F32)).astype(BF16)

    def sum_pass(array, k):
        part, size, ub, db, us, ur, ds, dr = array
        for i in range(Z - 1):
            d = Z - 1 - i

            def make_up(d=d):
                return copy(
                    part.at[k, pl.ds(d * size, size), :], ub.at[d, k], us.at[d, k], ur.at[d, k], z + 1, x, b
                )

            @pl.when(jnp.logical_and(z < d, z > 0))
            def _():
                make_up().wait_recv()
                add(array, k, d, ub.at[d, k])

            send_if(z < d, make_up)
            d = i

            def make_down(d=d):
                return copy(
                    part.at[k, pl.ds(d * size, size), :], db.at[d, k], ds.at[d, k], dr.at[d, k], z - 1, x, b
                )

            @pl.when(jnp.logical_and(z > d, z < Z - 1))
            def _():
                make_down().wait_recv()
                add(array, k, d, db.at[d, k])

            send_if(z > d, make_down)

    def sum_end(array, k, total):
        part, size, ub, db, us, ur, ds, dr = array
        mine = part.at[k, rows(z, size), :]
        total[...] = mine[...].astype(F32)

        @pl.when(z > 0)
        def _():
            copy(mine, ub.at[z, k], us.at[z, k], ur.at[z, k], z - 1, x, b).wait_recv()
            total[...] += ub[z, k].astype(F32)

        @pl.when(z < Z - 1)
        def _():
            copy(mine, db.at[z, k], ds.at[z, k], dr.at[z, k], z + 1, x, b).wait_recv()
            total[...] += db[z, k].astype(F32)

    barrier = pltpu.get_barrier_semaphore()

    def greet(zd, xd, bd):
        pl.semaphore_signal(barrier, inc=1, device_id=(zd * X + xd, bd), device_id_type=MESH)

    pl.when(z > 0)(lambda: greet(z - 1, x, b))
    pl.when(z < Z - 1)(lambda: greet(z + 1, x, b))
    for o in range(1, X):
        greet(z, xat(o), b)
    for k in range(1, L):
        greet(z, x, flip(k))
    wi[:, rows_1, :] = wi_ref[x]
    wo[:, rows(z, R2), :] = wo_ref[...]
    xg[0, rows_t, :] = x_ref[...]
    cg[rows_t, :] = ct_ref[...]
    inside = jnp.logical_and(z > 0, z < Z - 1)
    peers = X - 1 + L - 1
    pl.when(inside)(lambda: pl.semaphore_wait(barrier, peers + 2))
    pl.when(jnp.logical_not(inside))(lambda: pl.semaphore_wait(barrier, peers + 1))

    wx_c = [
        [
            send(wi_ref.at[xat(o), k], wi.at[k, rows_1, :], wx_s.at[o, k], wx_r.at[o, k], z, xat(o), b)
            for o in range(1, X)
        ]
        for k in range(L)
    ]
    xx_c = [send(x_ref, xg.at[0, rows_t, :], xx_s.at[o], xx_r.at[o], z, xat(o), b) for o in range(1, X)]
    x_c = [
        send(x_ref, xg.at[k, rows_t, :], x_s.at[k, 0], x_r.at[k, 0], z, x, flip(k))
        for k in reversed(range(1, L))
    ]
    for k in range(L):
        for c in wx_c[k]:
            c.wait_recv()
        gather_start(WI, k)
    for o in range(1, X):
        xx_c[o - 1].wait_recv()
        theirs = rows((x + X - o) % X, T)
        for k in reversed(range(1, L)):
            x_c.append(
                send(xg.at[0, theirs, :], xg.at[k, theirs, :], x_s.at[k, o], x_r.at[k, o], z, x, flip(k))
            )
    ct_c = [send(ct_ref, cg.at[rows_t, :], ct_s.at[o], ct_r.at[o], z, xat(o), b) for o in range(1, X)]
    for k in range(L):
        gather_pass(WI, k)
    back_order = list(reversed(range(L)))
    for k in back_order:
        gather_start(WO, k)
    for c in x_c:
        c.wait_recv()
    for k in range(L):
        gather_end(WI, k)

    def activate(r):
        v = dot(xg[0, r, :], wi[0], 1, 0)
        for k in range(1, L):
            v = v + dot(xg[k, r, :], wi[k], 1, 0)
        pa[r, :] = v
        t = jnp.tanh(GELU_C * v * (1.0 + GELU_A * (v * v)))
        hg[0, r, :] = (v * (0.5 + 0.5 * t)).astype(BF16)

    tiles(TX, 128, activate)
    hg_c = [
        send(hg.at[0], hg.at[k], hg_s.at[k], hg_r.at[k], z, x, flip(k))
        for k in reversed(range(1, L))
    ]
    gather_pass(WO, back_order[0])
    for c in ct_c:
        c.wait_recv()

    def grad_out(k):
        def one(r):
            go_part[k, r, :] = dot(hg[k, :, r], cg[...], 0, 0).astype(BF16)

        if k:
            hg_c[L - 1 - k].wait_recv()
        tiles(HX, 256, one)

    def hid_term(k):
        def one(r):
            term = dot(cg[r, :], wo[k], 1, 1).astype(BF16)
            if k:
                ht_send[k - 1, r, :] = term
            else:
                ht_own[r, :] = term

        gather_end(WO, k)
        tiles(TX, 256, one)
        if k:
            ht_c.append(send(ht_send.at[k - 1], ht_recv.at[k - 1], ht_s.at[k], ht_r.at[k], z, x, flip(k)))

    ht_c = []
    grad_out(0)
    for j, k in enumerate(back_order):
        if j + 1 < L:
            gather_pass(WO, back_order[j + 1])
        hid_term(k)
        if j + 1 < L:
            sum_pass(GO, j)
            grad_out(j + 1)

    for c in ht_c:
        c.wait_recv()

    def slope(r):
        g = ht_own[r, :].astype(F32)
        for k in range(1, L):
            g = g + ht_recv[k - 1, r, :].astype(F32)
        v = pa[r, :]
        v2 = v * v
        t = jnp.tanh(GELU_C * v * (1.0 + GELU_A * v2))
        d = 0.5 + 0.5 * t + 0.5 * v * (1.0 - t * t) * (GELU_C * (1.0 + 3.0 * GELU_A * v2))
        pg[r, :] = (g * d).astype(BF16)

    sum_pass(GO, L - 1)
    tiles(TX, 128, slope)

    def grad_in(k):
        def one(r):
            gi_part[k, r, :] = dot(xg[k, :, r], pg[...], 0, 0).astype(BF16)

        tiles(C, 256, one)

    ig_c = []

    def grad_x(k):
        def one(r):
            ig_send[k, r, :] = dot(pg[r, :], wi[k], 1, 1).astype(BF16)

        tiles(TX, 256, one)
        if k:
            ig_c.append(send(ig_send.at[k], ig_recv.at[k - 1], ig_s.at[k], ig_r.at[k], z, x, flip(k)))

    grad_in(0)
    for j, k in enumerate(back_order):
        grad_x(k)
        if j + 1 < L:
            grad_in(j + 1)
        if j == 0:
            def forward(r):
                total = dot(hg[0, r, :], wo[0], 1, 0)
                for i in range(1, L):
                    total = total + dot(hg[i, r, :], wo[i], 1, 0)
                o_send[r, :] = total.astype(BF16)

        sum_pass(GI, j)
    tiles(TX, 256, forward)
    o_c = [
        send(o_send.at[rows(xat(o), T), :], o_recv.at[o], o_s.at[o], o_r.at[o], z, xat(o), b)
        for o in range(1, X)
    ]
    for c in ig_c:
        c.wait_recv()

    def add_terms(r):
        total = ig_send[0, r, :].astype(F32)
        for k in range(1, L):
            total = total + ig_recv[k - 1, r, :].astype(F32)
        ig_sum[r, :] = total.astype(BF16)

    tiles(TX, 128, add_terms)
    igx_c = [
        send(ig_sum.at[rows(xat(o), T), :], ig_x.at[o], igx_s.at[o], igx_r.at[o], z, xat(o), b)
        for o in range(1, X)
    ]
    for k in range(L):
        sum_end(GO, k, go_ref.at[k])

    gx_c = []
    for k in range(L):
        sum_end(GI, k, acc)
        gx_send[k] = acc[...].astype(BF16)
        gi_ref[x, k] = acc[rows(x, R1), :]
        for o in range(1, X):
            gx_c.append(
                send(gx_send.at[k, rows(xat(o), R1), :], gx_recv.at[o, k], gx_s.at[o, k], gx_r.at[o, k], z, xat(o), b)
            )
    for mine, theirs, copies, result in ((o_send, o_recv, o_c, out_ref), (ig_sum, ig_x, igx_c, ig_ref)):
        total = mine[rows_t, :].astype(F32)
        for o in range(1, X):
            copies[o - 1].wait_recv()
            total = total + theirs[o].astype(F32)
        result[...] = total.astype(BF16)
    for c in gx_c:
        c.wait_recv()
    for o in range(1, X):
        gi_ref[(x + X - o) % X] = gx_recv[o].astype(F32)
    for done in sent:
        done()


def body(Z, X, inputs, weight_in, weight_out, cotangent):
    T, C = inputs.shape
    R1, L, panel = weight_in.shape
    R2 = weight_out.shape[0]
    TX, HX, RX = X * T, Z * R2, X * R1
    wi = weight_in.reshape(R1, L, Z, X, R2).transpose(3, 1, 0, 2, 4).reshape(X, L, R1, HX)
    wo = weight_out.transpose(1, 0, 2)
    vmem = pl.BlockSpec(memory_space=pltpu.VMEM)

    def buf(*shape):
        return pltpu.VMEM(shape, BF16)

    def sems(*shape):
        return [pltpu.SemaphoreType.DMA(shape)] * 2

    flops = 12 * TX * HX * C * L
    out, ig, gi, go = pl.pallas_call(
        functools.partial(kernel, Z, X, L),
        out_shape=(
            jax.ShapeDtypeStruct((T, C), BF16),
            jax.ShapeDtypeStruct((T, C), BF16),
            jax.ShapeDtypeStruct((X, L, R1, HX), F32),
            jax.ShapeDtypeStruct((L, R2, C), F32),
        ),
        in_specs=[vmem] * 4,
        out_specs=(vmem,) * 4,
        scratch_shapes=[
            buf(L, HX, C), buf(L, C, HX), buf(L, TX, C), buf(TX, C), pltpu.VMEM((TX, HX), F32),
            buf(TX, HX), buf(L - 1, TX, HX), buf(L - 1, TX, HX), buf(L, TX, HX), buf(TX, HX),
            buf(L, C, HX), buf(Z, L, RX, HX), buf(Z, L, RX, HX), buf(L, RX, HX), buf(X, L, R1, HX),
            pltpu.VMEM((RX, HX), F32),
            buf(L, HX, C), buf(Z, L, R2, C), buf(Z, L, R2, C),
            buf(L, TX, C), buf(L - 1, TX, C), buf(TX, C), buf(X, T, C), buf(TX, C), buf(X, T, C),
            *sems(Z - 1, L), *sems(Z - 1, L), *sems(Z - 1, L), *sems(Z - 1, L),
            *sems(Z, L), *sems(Z, L), *sems(Z, L), *sems(Z, L),
            *sems(X, L), *sems(X, L), *sems(X), *sems(L, X), *sems(X), *sems(L), *sems(L), *sems(L),
            *sems(X), *sems(X),
        ],
        compiler_params=pltpu.CompilerParams(
            collective_id=0, has_side_effects=True, vmem_limit_bytes=60 * 2**20
        ),
        cost_estimate=pl.CostEstimate(flops=flops, bytes_accessed=8 * 2**20, transcendentals=TX * HX),
    )(inputs, cotangent, wi, wo)
    grad_in = gi.reshape(X, L, R1, Z, R2).transpose(2, 1, 3, 0, 4).reshape(R1, L, panel)
    return out, ig, grad_in, go.transpose(1, 0, 2)


def solution(mesh):
    n = mesh.shape["dp"]
    Z = 4 if n % 4 == 0 else n
    placed = (P("dp", "block"), P("dp", None, "block"), P("dp", None, "block"), P("dp", "block"))
    return jax.shard_map(
        functools.partial(body, Z, n // Z),
        mesh=mesh,
        in_specs=placed,
        out_specs=(
            P("dp", "block"),
            P("dp", "block"),
            P("dp", None, "block"),
            P("dp", None, "block"),
        ),
        check_vma=False,
    )
```

```python
import functools

import jax
import jax.numpy as jnp
from jax import lax
from jax.experimental import pallas as pl
from jax.experimental.pallas import tpu as pltpu
from jax.sharding import PartitionSpec as P

MESH = pl.DeviceIdType.MESH
F32, BF16 = jnp.float32, jnp.bfloat16
GELU_C, GELU_A = 0.7978845608028654, 0.044715


def dot(a, b, ca, cb):
    return lax.dot_general(a, b, (((ca,), (cb,)), ((), ())), preferred_element_type=F32)


def tiles(total, size, step):
    size = min(size, total)

    def one(i, carry):
        step(pl.ds(pl.multiple_of(i * size, size), size))
        return carry

    lax.fori_loop(0, total // size, one, 0)


def kernel(
    Z, X, L, x_ref, ct_ref, wi_ref, wo_ref, out_ref, ig_ref, gi_ref, go_ref,
    wo, wi, xg, cg, pa, ht_own, ht_send, ht_recv, hg, pg, gi_part, gi_up, gi_dn, gx_send, gx_recv, acc,
    go_part, go_up, go_dn, ig_send, ig_recv, ig_sum, ig_x, o_send, o_recv,
    wo_us, wo_ur, wo_ds, wo_dr, wi_us, wi_ur, wi_ds, wi_dr, gi_us, gi_ur, gi_ds, gi_dr, go_us, go_ur, go_ds, go_dr,
    wx_s, wx_r, gx_s, gx_r, xx_s, xx_r, x_s, x_r, ct_s, ct_r, ht_s, ht_r, hg_s, hg_r, ig_s, ig_r, igx_s, igx_r, o_s, o_r,
):
    dp, b = lax.axis_index("dp"), lax.axis_index("block")
    z, x = dp // X, dp % X
    T, C = x_ref.shape
    R1, R2 = wi_ref.shape[2], wo_ref.shape[1]
    TX, HX, RX = X * T, Z * R2, X * R1

    def flip(k):
        d = 2 ** (k - 1)
        return b + d - 2 * d * ((b // d) % 2)

    def xat(o):
        return (x + o) % X

    def rows(index, size):
        return pl.ds(pl.multiple_of(index * size, size), size)

    rows_t = rows(x, T)
    rows_1 = rows(dp, R1)

    def copy(src, dst, ssem, rsem, zd, xd, bd):
        return pltpu.make_async_remote_copy(
            src_ref=src, dst_ref=dst, send_sem=ssem, recv_sem=rsem,
            device_id=(zd * X + xd, bd), device_id_type=MESH,
        )

    sent = []

    def send(*args):
        c = copy(*args)
        c.start()
        sent.append(c.wait_send)
        return c

    def send_if(cond, make):
        @pl.when(cond)
        def _():
            make().start()

        def done():
            @pl.when(cond)
            def _():
                make().wait_send()

        sent.append(done)

    WI = (wi, RX, wi_us, wi_ur, wi_ds, wi_dr)
    WO = (wo, R2, wo_us, wo_ur, wo_ds, wo_dr)

    def block(array, k, zz):
        return array[0].at[k, rows(zz, array[1]), :]

    def up(array, k, s):
        _, _, us, ur, _, _ = array
        send_if(
            jnp.logical_and(z >= s, z < Z - 1),
            lambda: copy(block(array, k, z - s), block(array, k, z - s), us.at[s, k], ur.at[s, k], z + 1, x, b),
        )

    def down(array, k, s):
        _, _, _, _, ds, dr = array
        send_if(
            jnp.logical_and(z + s < Z, z > 0),
            lambda: copy(block(array, k, z + s), block(array, k, z + s), ds.at[s, k], dr.at[s, k], z - 1, x, b),
        )

    def from_below(array, k, s):
        _, _, us, ur, _, _ = array

        @pl.when(z >= s + 1)
        def _():
            here = block(array, k, z - 1 - s)
            copy(here, here, us.at[s, k], ur.at[s, k], z - 1, x, b).wait_recv()

    def from_above(array, k, s):
        _, _, _, _, ds, dr = array

        @pl.when(z + 1 + s < Z)
        def _():
            here = block(array, k, z + 1 + s)
            copy(here, here, ds.at[s, k], dr.at[s, k], z + 1, x, b).wait_recv()

    def gather_start(array, k):
        up(array, k, 0)
        down(array, k, 0)

    def gather_pass(array, k):
        for s in range(Z - 2):
            from_below(array, k, s)
            up(array, k, s + 1)
            from_above(array, k, s)
            down(array, k, s + 1)

    def gather_end(array, k):
        from_below(array, k, Z - 2)
        from_above(array, k, Z - 2)

    GI = (gi_part, RX, gi_up, gi_dn, gi_us, gi_ur, gi_ds, gi_dr)
    GO = (go_part, R2, go_up, go_dn, go_us, go_ur, go_ds, go_dr)

    def add(array, k, d, here):
        part, size = array[0], array[1]
        r = pl.ds(d * size, size)
        part[k, r, :] = (part[k, r, :].astype(F32) + here[...].astype(F32)).astype(BF16)

    low = z < Z // 2

    def sum_up(array, k, half):
        part, size, ub, _, us, ur, _, _ = array
        for d in reversed(range(1, Z)):

            def make(d=d):
                return copy(
                    part.at[k, pl.ds(d * size, size), :], ub.at[d, k], us.at[d, k], ur.at[d, k], z + 1, x, b
                )

            @pl.when(jnp.logical_and(half, jnp.logical_and(z < d, z > 0)))
            def _():
                make().wait_recv()
                add(array, k, d, ub.at[d, k])

            send_if(jnp.logical_and(half, z < d), make)

    def sum_down(array, k, half):
        part, size, _, db, _, _, ds, dr = array
        for d in range(Z - 1):

            def make(d=d):
                return copy(
                    part.at[k, pl.ds(d * size, size), :], db.at[d, k], ds.at[d, k], dr.at[d, k], z - 1, x, b
                )

            @pl.when(jnp.logical_and(half, jnp.logical_and(z > d, z < Z - 1)))
            def _():
                make().wait_recv()
                add(array, k, d, db.at[d, k])

            send_if(jnp.logical_and(half, z > d), make)

    def sum_near(array, k):
        sum_up(array, k, low)
        sum_down(array, k, jnp.logical_not(low))

    def sum_far(array, k):
        sum_down(array, k, low)
        sum_up(array, k, jnp.logical_not(low))

    def sum_end(array, k, total):
        part, size, ub, db, us, ur, ds, dr = array
        mine = part.at[k, rows(z, size), :]
        total[...] = mine[...].astype(F32)

        @pl.when(z > 0)
        def _():
            copy(mine, ub.at[z, k], us.at[z, k], ur.at[z, k], z - 1, x, b).wait_recv()
            total[...] += ub[z, k].astype(F32)

        @pl.when(z < Z - 1)
        def _():
            copy(mine, db.at[z, k], ds.at[z, k], dr.at[z, k], z + 1, x, b).wait_recv()
            total[...] += db[z, k].astype(F32)

    barrier = pltpu.get_barrier_semaphore()

    def greet(zd, xd, bd):
        pl.semaphore_signal(barrier, inc=1, device_id=(zd * X + xd, bd), device_id_type=MESH)

    pl.when(z > 0)(lambda: greet(z - 1, x, b))
    pl.when(z < Z - 1)(lambda: greet(z + 1, x, b))
    for o in range(1, X):
        greet(z, xat(o), b)
    for k in range(1, L):
        greet(z, x, flip(k))
    wi[:, rows_1, :] = wi_ref[x]
    wo[:, rows(z, R2), :] = wo_ref[...]
    xg[0, rows_t, :] = x_ref[...]
    cg[rows_t, :] = ct_ref[...]
    inside = jnp.logical_and(z > 0, z < Z - 1)
    peers = X - 1 + L - 1
    pl.when(inside)(lambda: pl.semaphore_wait(barrier, peers + 2))
    pl.when(jnp.logical_not(inside))(lambda: pl.semaphore_wait(barrier, peers + 1))

    wx_c = [
        [
            send(wi_ref.at[xat(o), k], wi.at[k, rows_1, :], wx_s.at[o, k], wx_r.at[o, k], z, xat(o), b)
            for o in range(1, X)
        ]
        for k in range(L)
    ]
    xx_c = [send(x_ref, xg.at[0, rows_t, :], xx_s.at[o], xx_r.at[o], z, xat(o), b) for o in range(1, X)]
    x_c = [
        send(x_ref, xg.at[k, rows_t, :], x_s.at[k, 0], x_r.at[k, 0], z, x, flip(k))
        for k in reversed(range(1, L))
    ]
    for k in range(L):
        for c in wx_c[k]:
            c.wait_recv()
        gather_start(WI, k)
    for o in range(1, X):
        xx_c[o - 1].wait_recv()
        theirs = rows((x + X - o) % X, T)
        for k in reversed(range(1, L)):
            x_c.append(
                send(xg.at[0, theirs, :], xg.at[k, theirs, :], x_s.at[k, o], x_r.at[k, o], z, x, flip(k))
            )
    ct_c = [send(ct_ref, cg.at[rows_t, :], ct_s.at[o], ct_r.at[o], z, xat(o), b) for o in range(1, X)]
    for k in range(L):
        gather_pass(WI, k)
    back_order = list(reversed(range(L)))
    for k in back_order:
        gather_start(WO, k)
    for c in x_c:
        c.wait_recv()
    for k in range(L):
        gather_end(WI, k)

    def activate(r):
        v = dot(xg[0, r, :], wi[0], 1, 0)
        for k in range(1, L):
            v = v + dot(xg[k, r, :], wi[k], 1, 0)
        pa[r, :] = v
        t = jnp.tanh(GELU_C * v * (1.0 + GELU_A * (v * v)))
        hg[0, r, :] = (v * (0.5 + 0.5 * t)).astype(BF16)

    tiles(TX, 128, activate)
    hg_c = [
        send(hg.at[0], hg.at[k], hg_s.at[k], hg_r.at[k], z, x, flip(k))
        for k in reversed(range(1, L))
    ]
    gather_pass(WO, back_order[0])
    for c in ct_c:
        c.wait_recv()

    def grad_out(k):
        def one(r):
            go_part[k, r, :] = dot(hg[k, :, r], cg[...], 0, 0).astype(BF16)

        if k:
            hg_c[L - 1 - k].wait_recv()
        tiles(HX, 256, one)

    def hid_term(k):
        def one(r):
            term = dot(cg[r, :], wo[k], 1, 1).astype(BF16)
            if k:
                ht_send[k - 1, r, :] = term
            else:
                ht_own[r, :] = term

        gather_end(WO, k)
        tiles(TX, 256, one)
        if k:
            ht_c.append(send(ht_send.at[k - 1], ht_recv.at[k - 1], ht_s.at[k], ht_r.at[k], z, x, flip(k)))

    ht_c = []
    grad_out(0)
    for j, k in enumerate(back_order):
        if j + 1 < L:
            gather_pass(WO, back_order[j + 1])
        hid_term(k)
        if j + 1 < L:
            sum_near(GO, j)
            grad_out(j + 1)
        if j and j + 1 < L:
            sum_far(GO, j - 1)

    sum_near(GO, L - 1)
    sum_far(GO, L - 2)
    for c in ht_c:
        c.wait_recv()

    def slope(r):
        g = ht_own[r, :].astype(F32)
        for k in range(1, L):
            g = g + ht_recv[k - 1, r, :].astype(F32)
        v = pa[r, :]
        v2 = v * v
        t = jnp.tanh(GELU_C * v * (1.0 + GELU_A * v2))
        d = 0.5 + 0.5 * t + 0.5 * v * (1.0 - t * t) * (GELU_C * (1.0 + 3.0 * GELU_A * v2))
        pg[r, :] = (g * d).astype(BF16)

    tiles(TX, 128, slope)

    def grad_in(k):
        def one(r):
            gi_part[k, r, :] = dot(xg[k, :, r], pg[...], 0, 0).astype(BF16)

        tiles(C, 256, one)

    ig_c = []

    def grad_x(k):
        def one(r):
            ig_send[k, r, :] = dot(pg[r, :], wi[k], 1, 1).astype(BF16)

        tiles(TX, 256, one)
        if k:
            ig_c.append(send(ig_send.at[k], ig_recv.at[k - 1], ig_s.at[k], ig_r.at[k], z, x, flip(k)))

    grad_in(0)
    sum_near(GI, 0)
    sum_far(GO, L - 1)
    for j, k in enumerate(back_order):
        grad_x(k)
        if j + 1 < L:
            grad_in(j + 1)
            sum_near(GI, j + 1)
        if j == 0:
            def forward(r):
                total = dot(hg[0, r, :], wo[0], 1, 0)
                for i in range(1, L):
                    total = total + dot(hg[i, r, :], wo[i], 1, 0)
                o_send[r, :] = total.astype(BF16)

        sum_far(GI, j)
    tiles(TX, 256, forward)
    o_c = [
        send(o_send.at[rows(xat(o), T), :], o_recv.at[o], o_s.at[o], o_r.at[o], z, xat(o), b)
        for o in range(1, X)
    ]
    for c in ig_c:
        c.wait_recv()

    def add_terms(r):
        total = ig_send[0, r, :].astype(F32)
        for k in range(1, L):
            total = total + ig_recv[k - 1, r, :].astype(F32)
        ig_sum[r, :] = total.astype(BF16)

    tiles(TX, 128, add_terms)
    igx_c = [
        send(ig_sum.at[rows(xat(o), T), :], ig_x.at[o], igx_s.at[o], igx_r.at[o], z, xat(o), b)
        for o in range(1, X)
    ]
    for k in range(L):
        sum_end(GO, k, go_ref.at[k])

    gx_c = []
    for k in range(L):
        sum_end(GI, k, acc)
        gx_send[k] = acc[...].astype(BF16)
        gi_ref[x, k] = acc[rows(x, R1), :]
        for o in range(1, X):
            gx_c.append(
                send(gx_send.at[k, rows(xat(o), R1), :], gx_recv.at[o, k], gx_s.at[o, k], gx_r.at[o, k], z, xat(o), b)
            )
    for mine, theirs, copies, result in ((o_send, o_recv, o_c, out_ref), (ig_sum, ig_x, igx_c, ig_ref)):
        total = mine[rows_t, :].astype(F32)
        for o in range(1, X):
            copies[o - 1].wait_recv()
            total = total + theirs[o].astype(F32)
        result[...] = total.astype(BF16)
    for c in gx_c:
        c.wait_recv()
    for o in range(1, X):
        gi_ref[(x + X - o) % X] = gx_recv[o].astype(F32)
    for done in sent:
        done()


def body(Z, X, inputs, weight_in, weight_out, cotangent):
    T, C = inputs.shape
    R1, L, panel = weight_in.shape
    R2 = weight_out.shape[0]
    TX, HX, RX = X * T, Z * R2, X * R1
    wi = weight_in.reshape(R1, L, Z, X, R2).transpose(3, 1, 0, 2, 4).reshape(X, L, R1, HX)
    wo = weight_out.transpose(1, 0, 2)
    vmem = pl.BlockSpec(memory_space=pltpu.VMEM)

    def buf(*shape):
        return pltpu.VMEM(shape, BF16)

    def sems(*shape):
        return [pltpu.SemaphoreType.DMA(shape)] * 2

    flops = 12 * TX * HX * C * L
    out, ig, gi, go = pl.pallas_call(
        functools.partial(kernel, Z, X, L),
        out_shape=(
            jax.ShapeDtypeStruct((T, C), BF16),
            jax.ShapeDtypeStruct((T, C), BF16),
            jax.ShapeDtypeStruct((X, L, R1, HX), F32),
            jax.ShapeDtypeStruct((L, R2, C), F32),
        ),
        in_specs=[vmem] * 4,
        out_specs=(vmem,) * 4,
        scratch_shapes=[
            buf(L, HX, C), buf(L, C, HX), buf(L, TX, C), buf(TX, C), pltpu.VMEM((TX, HX), F32),
            buf(TX, HX), buf(L - 1, TX, HX), buf(L - 1, TX, HX), buf(L, TX, HX), buf(TX, HX),
            buf(L, C, HX), buf(Z, L, RX, HX), buf(Z, L, RX, HX), buf(L, RX, HX), buf(X, L, R1, HX),
            pltpu.VMEM((RX, HX), F32),
            buf(L, HX, C), buf(Z, L, R2, C), buf(Z, L, R2, C),
            buf(L, TX, C), buf(L - 1, TX, C), buf(TX, C), buf(X, T, C), buf(TX, C), buf(X, T, C),
            *sems(Z - 1, L), *sems(Z - 1, L), *sems(Z - 1, L), *sems(Z - 1, L),
            *sems(Z, L), *sems(Z, L), *sems(Z, L), *sems(Z, L),
            *sems(X, L), *sems(X, L), *sems(X), *sems(L, X), *sems(X), *sems(L), *sems(L), *sems(L),
            *sems(X), *sems(X),
        ],
        compiler_params=pltpu.CompilerParams(
            collective_id=0, has_side_effects=True, vmem_limit_bytes=60 * 2**20
        ),
        cost_estimate=pl.CostEstimate(flops=flops, bytes_accessed=8 * 2**20, transcendentals=TX * HX),
    )(inputs, cotangent, wi, wo)
    grad_in = gi.reshape(X, L, R1, Z, R2).transpose(2, 1, 3, 0, 4).reshape(R1, L, panel)
    return out, ig, grad_in, go.transpose(1, 0, 2)


def solution(mesh):
    n = mesh.shape["dp"]
    Z = 4 if n % 4 == 0 else n
    placed = (P("dp", "block"), P("dp", None, "block"), P("dp", None, "block"), P("dp", "block"))
    return jax.shard_map(
        functools.partial(body, Z, n // Z),
        mesh=mesh,
        in_specs=placed,
        out_specs=(
            P("dp", "block"),
            P("dp", "block"),
            P("dp", None, "block"),
            P("dp", None, "block"),
        ),
        check_vma=False,
    )
```
